32 devices in a mesh: seq: 8 (over z, y), dp: 4 (over x, core).
Axes of the slice: x: 2, y: 2, z: 4, core: 2. Of those that a mesh axis runs over, the one named last changes fastest.
Arguments:
- tokens: bfloat16 [4, 1024, 1536], P('dp', 'seq'), may hold values from -6 to 6
- w_in: bfloat16 [1536, 1536], P('dp'), may hold values from -0.15625 to 0.15625
- w_out: bfloat16 [1536, 1536], P('dp'), may hold values from -0.15625 to 0.15625
- first_factor: bfloat16 [8, 128, 128], P('seq'), may hold values from -0.5 to 0.5
- second_factor: bfloat16 [128, 8, 8], P('seq'), may hold values from -2 to 2
- cotangent: bfloat16 [4, 1024, 1536], P('dp', 'seq'), may hold values from -6 to 6
Outputs:
- mixed: bfloat16 [4, 1024, 1536], P('dp', 'seq')
- input_grad: bfloat16 [4, 1024, 1536], P('dp', 'seq')
- out_weight_grad: float32 [1536, 1536], P(('seq', 'dp'))
The draws below stay inside these ranges and needn't reach their ends.
All inputs are finite; a program needn't handle non-finite values.
Results may differ from the reference program's by a relative error of at most 0.0071.
Values may be sent and summed in bfloat16 or wider, within the bound.
No kernel may reach another device: no remote copies, remote signals or barrier semaphores. Data moves between devices by JAX's collectives and lax.ppermute only.
A program may use at most 128 MiB of HBM per device.

```python
import jax
import jax.numpy as jnp
from jax import lax

D = 1536
BLOCK = 128
LENGTH = 1024
SPAN = 8
SEQS = 4


def level_of(rng, extent, cuts, least, top_value):
    level = 1.0
    for axis_at, parts in cuts:
        heights = jax.random.uniform(jax.random.fold_in(jax.random.fold_in(rng, 6), axis_at), (parts,), jnp.float32, least / len(cuts), top_value / len(cuts))
        level = level * jnp.repeat(jnp.exp(heights), extent[axis_at] // parts).reshape((-1,) + (1,) * (len(extent) - 1 - axis_at))
    return level


def gaussian(rng, dims, deviation, most, cuts=(), held_as=jnp.bfloat16):
    drawn = jax.random.normal(rng, dims, jnp.float32) * deviation
    if len(cuts) > 0:
        drawn = level_of(rng, dims, cuts, -0.22, 0.18) * drawn
    return jnp.clip(drawn, min=-most, max=most).astype(held_as)


def setup_inputs(seed: int = 0) -> dict:
    key_list = jax.random.split(jax.random.key(seed), 7)
    tokens = gaussian(key_list[0], (SEQS, LENGTH, D), 1.0, 6.0, ((0, 4), (1, 8)))
    w_in = gaussian(key_list[1], (D, D), D ** -0.5, 0.15625, ((0, 4),))
    w_out = gaussian(key_list[2], (D, D), D ** -0.5, 0.15625, ((0, 4),))
    first_factor = gaussian(key_list[3], (SPAN, BLOCK, BLOCK), BLOCK ** -0.5, 0.5, ((0, 8),))
    second_factor = gaussian(key_list[4], (BLOCK, SPAN, SPAN), SPAN ** -0.5, 2.0, ((0, 8),))
    cotangent = gaussian(key_list[5], (SEQS, LENGTH, D), 1.0, 6.0, ((0, 4), (1, 8)))
    return dict(tokens=tokens, w_in=w_in, w_out=w_out, first_factor=first_factor, second_factor=second_factor, cotangent=cotangent)


def mixer_forward(projected, first_factor, second_factor):
    blocks = projected.reshape(SPAN, BLOCK, D).astype(jnp.float32)
    first_mix = jnp.einsum('bst,btd->bsd', first_factor.astype(jnp.float32), blocks).astype(jnp.bfloat16)
    second = jnp.einsum('sab,bsd->asd', second_factor.astype(jnp.float32), first_mix.astype(jnp.float32))
    return second.astype(jnp.bfloat16).reshape(LENGTH, D)

def mixer_backward(monarch_grad, first_factor, second_factor):
    blocks = monarch_grad.reshape(SPAN, BLOCK, D).astype(jnp.float32)
    first_grad = jnp.einsum('sab,asd->bsd', second_factor.astype(jnp.float32), blocks).astype(jnp.bfloat16)
    back = jnp.einsum('bst,bsd->btd', first_factor.astype(jnp.float32), first_grad.astype(jnp.float32))
    return back.astype(jnp.bfloat16).reshape(LENGTH, D)

def reference(tokens, w_in, w_out, first_factor, second_factor, cotangent):
    outputs = []
    grads = []
    weight_grad = jnp.zeros((D, D), jnp.float32)
    for index in range(SEQS):
        inputs = tokens[index]
        upstream = cotangent[index]
        projected = jnp.dot(inputs, w_in, preferred_element_type=jnp.float32).astype(jnp.bfloat16)
        monarch = mixer_forward(projected, first_factor, second_factor)
        inputs_wide = inputs.astype(jnp.float32)
        sigma = jax.nn.sigmoid(inputs_wide)
        gate = jax.nn.silu(inputs_wide)
        gated = (monarch.astype(jnp.float32) * gate).astype(jnp.bfloat16)
        outputs.append(jnp.dot(gated, w_out, preferred_element_type=jnp.float32).astype(jnp.bfloat16))
        gated_grad = jnp.dot(upstream, w_out.T, preferred_element_type=jnp.float32)
        monarch_grad = (gated_grad * gate).astype(jnp.bfloat16)
        projected_grad = mixer_backward(monarch_grad, first_factor, second_factor)
        gate_term = gated_grad * monarch.astype(jnp.float32) * (sigma * (1.0 + inputs_wide * (1.0 - sigma)))
        total = jnp.dot(projected_grad, w_in.T, preferred_element_type=jnp.float32) + gate_term
        grads.append(total.astype(jnp.bfloat16))
        weight_grad = weight_grad + lax.dot_general(gated, upstream, (((0,), (0,)), ((), ())), preferred_element_type=jnp.float32)
    weight_grad = weight_grad / jnp.sqrt(jnp.float32(SEQS * LENGTH))
    return (jnp.stack(outputs), jnp.stack(grads), weight_grad)
```

```python
import jax
import jax.numpy as jnp
from jax import lax
from jax.sharding import PartitionSpec as P

F32 = jnp.float32
BF16 = jnp.bfloat16


def dot(a, b, ca, cb):
    return lax.dot_general(a, b, (((ca,), (cb,)), ((), ())), preferred_element_type=F32)


def swap(x, axis, bit):
    n = lax.axis_size(axis)
    return lax.ppermute(x, axis, [(i, i ^ bit) for i in range(n)])


def everywhere(x):
    far = swap(x, "dp", 2)
    return x, swap(x, "dp", 1), far, swap(far, "dp", 1)


def spread(x):
    return lax.all_to_all(x, "seq", split_axis=0, concat_axis=0, tiled=True)


def on_device(tokens, w_in, w_out, first_factor, second_factor, cotangent):
    inputs = tokens[0]
    upstream = cotangent[0]
    first = first_factor[0]
    rows, width = inputs.shape
    nseq = lax.axis_size("seq")
    ndp = lax.axis_size("dp")
    me = lax.axis_index("dp")
    my_s = lax.axis_index("seq")
    part = width // ndp
    offs = rows // nseq
    outer = nseq // 2
    piece = width // (nseq * ndp)

    def columns(x, r):
        return lax.dynamic_slice_in_dim(x, (me ^ r) * part, part, axis=1)

    mix = dot(first, inputs, 1, 0).astype(BF16).reshape(nseq, offs, width)
    mix = spread(mix)
    mix = jnp.einsum("sab,bsd->asd", second_factor, mix, preferred_element_type=F32).astype(BF16)
    mix = spread(mix).reshape(rows, width)

    cots = everywhere(upstream)
    toward = jnp.concatenate([columns(inputs, 2), columns(inputs, 3)], axis=1)
    toward = swap(toward, "dp", 2)
    side = swap(jnp.concatenate([columns(inputs, 1), toward[:, part:]], axis=1), "dp", 1)
    mine = (columns(inputs, 0), side[:, :part], toward[:, :part], side[:, part:])

    grads = []
    for cot, tok in zip(cots, mine):
        gate = jax.nn.silu(tok.astype(F32))
        grads.append((dot(cot, w_out, 1, 1) * gate).astype(BF16))
    grads = jnp.stack(grads)
    grads = jnp.stack(
        [lax.dynamic_index_in_dim(grads, me ^ j, 0, keepdims=False) for j in range(ndp)]
    )
    grads = grads.reshape(ndp, nseq, offs, part).transpose(1, 0, 2, 3)
    grads = grads.reshape(nseq * ndp, offs, part)
    grads = lax.all_to_all(grads, ("seq", "dp"), split_axis=0, concat_axis=0, tiled=True)
    grads = grads.reshape(nseq, ndp, offs, part)
    back = jnp.einsum("sab,ajsc->bjsc", second_factor, grads, preferred_element_type=F32)
    back = spread(back.astype(BF16))
    back = back.transpose(0, 2, 1, 3).reshape(rows, width)
    back = dot(first, back, 0, 0).astype(BF16)

    w_ins = everywhere(w_in)
    w_outs = everywhere(w_out)

    wide = inputs.astype(F32)
    gate = jax.nn.silu(wide)
    monarch = sum(dot(columns(mix, r), w_ins[r], 1, 0) for r in range(ndp))
    monarch = monarch.astype(BF16)
    gated = (monarch.astype(F32) * gate).astype(BF16)

    pairs = [upstream, cots[2]]
    other = [swap(c, "seq", 1) for c in pairs]
    quad = [pairs[0], cots[1], pairs[1], cots[3]]
    far = [other[0], swap(other[0], "dp", 1), other[1], swap(other[1], "dp", 1)]
    send = gated.T.reshape(outer, 2 * ndp, piece, rows).transpose(1, 0, 2, 3)
    groups = [[z * 2 * ndp + i for i in range(2 * ndp)] for z in range(outer)]
    got = lax.all_to_all(
        send, ("seq", "dp"), split_axis=0, concat_axis=0, tiled=True, axis_index_groups=groups
    )
    got = got.reshape(2 * ndp, outer * piece, rows)
    here = (my_s % 2) * ndp + me
    total = 0.0
    for r, cot in enumerate(quad + far):
        total = total + dot(lax.dynamic_index_in_dim(got, here ^ r, 0, keepdims=False), cot, 1, 0)
    total = total.astype(BF16).reshape(outer, piece, width)
    lines = [[2 * z + y for z in range(outer)] for y in range(2)]
    total = lax.all_to_all(
        total, "seq", split_axis=0, concat_axis=0, tiled=True, axis_index_groups=lines
    )
    total = jnp.sum(total.astype(F32), axis=0)
    weight_grad = total / jnp.sqrt(F32(rows * nseq * ndp))

    mixed = sum(dot(columns(gated, r), w_outs[r], 1, 0) for r in range(ndp)).astype(BF16)
    out = []
    for r in range(ndp):
        x = columns(wide, r)
        sigma = jax.nn.sigmoid(x)
        slope = sigma * (1.0 + x * (1.0 - sigma))
        term = dot(upstream, w_outs[r], 1, 1) * columns(monarch, r).astype(F32) * slope
        out.append((dot(back, w_ins[r], 1, 1) + term).astype(BF16))
    out = jnp.concatenate(out, axis=1)
    input_grad = jnp.concatenate(
        [lax.dynamic_slice_in_dim(out, (me ^ j) * part, part, axis=1) for j in range(ndp)], axis=1
    )
    return mixed[None], input_grad[None], weight_grad


def solution(mesh):
    placed = (
        P("dp", "seq", None),
        P("dp", None),
        P("dp", None),
        P("seq", None, None),
        P("seq", None, None),
        P("dp", "seq", None),
    )
    return jax.shard_map(
        on_device,
        mesh=mesh,
        in_specs=placed,
        out_specs=(P("dp", "seq", None), P("dp", "seq", None), P(("seq", "dp"), None)),
        check_vma=False,
    )
```

```python
import functools

import jax
import jax.numpy as jnp
from jax import lax
from jax.experimental import pallas as pl
from jax.experimental.pallas import tpu as pltpu
from jax.sharding import PartitionSpec as P

F32 = jnp.float32
BF16 = jnp.bfloat16
VMEM = pl.BlockSpec(memory_space=pltpu.VMEM)
SMEM = pl.BlockSpec(memory_space=pltpu.SMEM)
MIB = 1024 * 1024


def dot(a, b, ca, cb):
    return lax.dot_general(a, b, (((ca,), (cb,)), ((), ())), preferred_element_type=F32)


def swap(x, axis, bit):
    n = lax.axis_size(axis)
    return lax.ppermute(x, axis, [(i, i ^ bit) for i in range(n)])


def after(x, *others):
    return lax.optimization_barrier((x, others))[0]


def relative(x, index):
    bit = 1
    while bit < x.shape[0]:
        flipped = x.reshape((-1, 2, bit) + x.shape[1:])[:, ::-1].reshape(x.shape)
        x = jnp.where(index & bit != 0, flipped, x)
        bit *= 2
    return x


def spread(x):
    return lax.all_to_all(x, "seq", split_axis=0, concat_axis=0, tiled=True)


def aligned(start, step):
    return pl.multiple_of(start * step, step)


def call(kernel, outs, *args, flops=0, scratch=(), room=60):
    nbytes = sum(x.size * x.dtype.itemsize for x in args + tuple(outs))
    return pl.pallas_call(
        kernel,
        out_shape=list(outs),
        in_specs=[SMEM if x.dtype == jnp.int32 else VMEM for x in args],
        out_specs=[VMEM] * len(outs),
        scratch_shapes=list(scratch),
        compiler_params=pltpu.CompilerParams(vmem_limit_bytes=room * MIB),
        cost_estimate=pl.CostEstimate(flops=flops, bytes_accessed=nbytes, transcendentals=0),
    )(*args)


def shape(dims, dtype=BF16):
    return jax.ShapeDtypeStruct(dims, dtype)


def grad_kernel(part, where, w, tok, cot, near, far, side, *refs):
    me = where[0]
    width = cot.shape[1]
    out = refs[-1]
    if len(refs) > 1:
        out[:, :, 0] = refs[0][...]
    pairs = (
        (cot[...], tok[:, pl.ds(aligned(me, part), part)]),
        (near[:, :width], near[:, width:]),
        (far[:, part : part + width], far[:, :part]),
        (side[:, part : part + width], side[:, part + width :]),
    )
    for r, (x, t) in enumerate(pairs):
        grad = (dot(x, w[...], 1, 1) * jax.nn.silu(t.astype(F32))).astype(BF16)
        if len(refs) > 1:
            offs = out.shape[3]
            for s in range(out.shape[0]):
                out[s, me ^ r, 1] = grad[s * offs : (s + 1) * offs]
        else:
            out[me ^ r] = grad


def gate_kernel(part, piece, tile, where, mix, w0, w1, w2, w3, tok, mon_out, gated_out, t_out, held):
    me, z = where[0], where[1]
    rows, width = tok.shape
    if len(mix.shape) == 5:
        lhs = [mix[:, pl.ds(me ^ r, 1), 0].reshape(rows, part) for r in range(4)]
    else:
        lhs = [mix[:, pl.ds(aligned(me ^ r, part), part)] for r in range(4)]
    for c in range(0, width, tile):
        cols = slice(c, c + tile)
        total = dot(lhs[0], w0[:, cols], 1, 0)
        for x, w in zip(lhs[1:], (w1, w2, w3)):
            total += dot(x, w[:, cols], 1, 0)
        mon = total.astype(BF16)
        mon_out[:, cols] = mon
        wide = tok[:, cols].astype(F32)
        gated = (mon.astype(F32) * jax.nn.silu(wide)).astype(BF16)
        gated_out[:, cols] = gated
        held[cols, :] = gated.T
    if len(t_out.shape) == 3:
        near, outer = t_out.shape[0], t_out.shape[1] // piece
        for i in range(near):
            for rel in range(outer):
                src = (rel ^ z) * near + i
                t_out[i, rel * piece : (rel + 1) * piece, :] = held[pl.ds(aligned(src, piece), piece), :]
    else:
        t_out[...] = held[...]


def carry_kernel(part, where, back, first, term, w0, w1, w2, w3, out):
    me = where[0]
    if len(back.shape) == 4:
        nseq, ndp, offs, _ = back.shape
        parts = [back[:, d].reshape(nseq * offs, part) for d in range(ndp)]
        back = jnp.concatenate(parts, axis=1)
    else:
        back = back[...]
    grad = dot(first[...], back, 0, 0).astype(BF16)
    for r, w in enumerate((w0, w1, w2, w3)):
        cols = pl.ds(aligned(me ^ r, part), part)
        out[:, cols] = (dot(grad, w[...], 1, 1) + term[:, cols]).astype(BF16)


def last_kernel(part, where, gated, mon, tok, cot, w0, w1, w2, w3, w4, w5, mixed, out):
    me = where[0]
    weights = (w0, w1, w2, w3, w4, w5)
    half = part // 2
    for r, some in enumerate(((w0,), (w1,), (w2, w3), (w4, w5))):
        cols = pl.ds(aligned(me ^ r, part), part)
        wide = tok[:, cols].astype(F32)
        sigma = jax.nn.sigmoid(wide)
        slope = sigma * (1.0 + wide * (1.0 - sigma))
        grad = jnp.concatenate([dot(cot[...], w[...], 1, 1) for w in some], axis=1)
        out[:, cols] = grad * mon[:, cols].astype(F32) * slope
    lhs = [gated[:, pl.ds(aligned(me ^ r, part), part)] for r in range(4)]
    lhs = lhs[:2] + [x[:, h : h + half] for x in lhs[2:] for h in (0, half)]
    for c in range(0, mixed.shape[1], part):
        cols = slice(c, c + part)
        total = dot(lhs[0], w0[:, cols], 1, 0)
        for x, w in zip(lhs[1:], weights[1:]):
            total += dot(x, w[:, cols], 1, 0)
        mixed[:, cols] = total.astype(BF16)


def weight_kernel(tile, starts, where, got, *refs):
    cots, out = refs[: len(starts)], refs[len(starts) :]
    width = out[0].shape[-1]
    here = where[2]
    for c in range(0, width, tile):
        cols = slice(c, c + tile)
        total = 0.0
        for r, (cot, start) in enumerate(zip(cots, starts)):
            total += dot(got[here ^ r], cot[:, c + start : c + start + tile], 1, 0)
        if len(out) == 1:
            out[0][:, cols] = total
            continue
        kept, sent = out
        n, piece, _ = kept.shape
        for i in range(n):
            kept[i, :, cols] = total[2 * i * piece : (2 * i + 1) * piece]
            sent[i, :, cols] = total[(2 * i + 1) * piece : (2 * i + 2) * piece].astype(BF16)


def on_device(tokens, w_in, w_out, first_factor, second_factor, cotangent):
    inputs = tokens[0]
    upstream = cotangent[0]
    first = first_factor[0]
    rows, width = inputs.shape
    nseq = lax.axis_size("seq")
    ndp = lax.axis_size("dp")
    me = lax.axis_index("dp")
    my_s = lax.axis_index("seq")
    flat = my_s * ndp + me
    part = width // ndp
    offs = rows // nseq
    piece = width // (nseq * ndp)
    flops = 2 * rows * width * width

    def columns(x, r):
        return lax.dynamic_slice_in_dim(x, (me ^ r) * part, part, axis=1)

    def unchunk(x):
        return x.transpose(0, 2, 1, 3).reshape(rows, width)

    def halve(x, bit, other=()):
        x = x.reshape(x.shape[0] // 2, 2, piece, width)
        got = swap(x[:, 1].astype(BF16), "seq", 2 * bit)
        got, other = lax.optimization_barrier((got, other))
        return x[:, 0] + got.astype(F32), other

    join = lax.optimization_barrier
    near = 2 * ndp
    outer = nseq // 2
    here = flat % near
    where = jnp.stack([me, flat // near, here]).astype(jnp.int32)

    def cut(x):
        return x.reshape(nseq, offs, ndp, part).transpose(0, 2, 1, 3)

    def exchange(x):
        flat_x = x.reshape((nseq * ndp,) + x.shape[2:])
        flat_x = lax.all_to_all(
            flat_x, ("seq", "dp"), split_axis=0, concat_axis=0, tiled=True
        )
        return flat_x.reshape(x.shape)

    cot_far = swap(jnp.concatenate([columns(inputs, 2), upstream, columns(inputs, 3)], axis=1), "dp", 2)
    cot_near = swap(jnp.concatenate([upstream, columns(inputs, 1)], axis=1), "dp", 1)
    mix, cot_near = join((dot(first, inputs, 1, 0).astype(BF16), cot_near))
    arrived = exchange(cut(mix))
    cot_side = swap(cot_far, "dp", 1)
    arrived, cot_near, cot_far, cot_side, w_late, up = join(
        (arrived, cot_near, cot_far, cot_side, w_in, upstream)
    )

    mix = jnp.einsum("sab,bjsd->ajsd", second_factor, arrived, preferred_element_type=F32)
    w_far = swap(w_late, "dp", 2)
    w_near = swap(w_late, "dp", 1)
    pair = jnp.concatenate([up, cot_far[:, part : part + width]], axis=1)
    pair = swap(pair, "seq", 1)
    pair_side = swap(pair, "dp", 1)
    w_side = swap(w_far, "dp", 1)
    mix = mix.astype(BF16)
    split = offs % 16 == 0 and piece % 16 == 0
    (both,) = call(
        functools.partial(grad_kernel, part),
        [shape((nseq, ndp, 2, offs, part) if split else (ndp, rows, part))],
        where,
        w_out,
        inputs,
        upstream,
        cot_near,
        cot_far,
        cot_side,
        *([mix] if split else []),
        flops=flops,
        room=40,
    )
    if not split:
        both = both.reshape(ndp, nseq, offs, part).transpose(1, 0, 2, 3)
        both = jnp.stack([mix, both], axis=2)
    both = exchange(both)
    both, w_far, w_near, w_side, pair, pair_side, w_late = join(
        (both, w_far, w_near, w_side, pair, pair_side, w_out)
    )
    out_a = swap(w_late[: part // 2], "dp", 2)
    out_b = swap(w_late[part // 2 :], "dp", 2)

    mix = both if split else unchunk(both[:, :, 0])
    back = jnp.einsum("sab,ajsc->bjsc", second_factor, both[:, :, 1], preferred_element_type=F32)
    back = back.astype(BF16)
    w_ins = (w_in, w_near, w_far, w_side)
    monarch, gated, turned = call(
        functools.partial(gate_kernel, part, piece, part),
        [
            shape((rows, width)),
            shape((rows, width)),
            shape((near, outer * piece, rows) if split else (width, rows)),
        ],
        where,
        mix,
        *w_ins,
        inputs,
        flops=flops,
        scratch=[pltpu.VMEM((width, rows), BF16)],
    )
    if not split:
        turned = relative(turned.reshape(outer, near, piece, rows), flat // near)
        turned = turned.transpose(1, 0, 2, 3).reshape(near, outer * piece, rows)
    groups = [[z * near + i for i in range(near)] for z in range(outer)]
    got = lax.all_to_all(
        turned, ("seq", "dp"), split_axis=0, concat_axis=0, tiled=True, axis_index_groups=groups
    )
    got, back, out_a = join((got, back, out_a))

    back = spread(back)
    halves = (outer // 2, piece, width)
    total = call(
        functools.partial(
            weight_kernel, part, (0, 0, part, part, 0, 0, width, width)
        ),
        [shape(halves, F32), shape(halves)] if split else [shape((outer * piece, width), F32)],
        where,
        got,
        upstream,
        cot_near,
        cot_far,
        cot_side,
        pair,
        pair_side,
        pair,
        pair_side,
        flops=flops,
    )
    if not split:
        total = total[0].reshape(outer // 2, 2, piece, width)
        total = (total[:, 0], total[:, 1].astype(BF16))
    kept, sent = total
    sent = swap(sent, "seq", 2)
    sent, back, out_b = join((sent, back, out_b))
    total = kept + sent.astype(F32)
    bit = 2

    w_outs = (
        w_out,
        swap(w_late, "dp", 1),
        out_a,
        out_b,
        swap(out_a, "dp", 1),
        swap(out_b, "dp", 1),
    )
    mixed, term = call(
        functools.partial(last_kernel, part),
        [shape((rows, width)), shape((rows, width), F32)],
        where,
        gated,
        monarch,
        inputs,
        upstream,
        *w_outs,
        flops=2 * flops,
        room=40,
    )
    if offs % 16 != 0:
        back = unchunk(back)
    (input_grad,) = call(
        functools.partial(carry_kernel, part),
        [shape((rows, width))],
        where,
        back,
        first,
        term,
        *w_ins,
        flops=flops,
        room=40,
    )
    ready = (mixed, input_grad)
    while total.shape[0] > 1:
        total, ready = halve(total, bit, ready)
        bit *= 2
    mixed, input_grad = ready
    weight_grad = total[0] / jnp.sqrt(F32(rows * nseq * ndp))
    return mixed[None], input_grad[None], weight_grad


def solution(mesh):
    placed = (
        P("dp", "seq", None),
        P("dp", None),
        P("dp", None),
        P("seq", None, None),
        P("seq", None, None),
        P("dp", "seq", None),
    )
    return jax.shard_map(
        on_device,
        mesh=mesh,
        in_specs=placed,
        out_specs=(P("dp", "seq", None), P("dp", "seq", None), P(("seq", "dp"), None)),
        check_vma=False,
    )
```

```python
import functools

import jax
import jax.numpy as jnp
from jax import lax
from jax.experimental import pallas as pl
from jax.experimental.pallas import tpu as pltpu
from jax.sharding import PartitionSpec as P

F32 = jnp.float32
BF16 = jnp.bfloat16
VMEM = pl.BlockSpec(memory_space=pltpu.VMEM)
SMEM = pl.BlockSpec(memory_space=pltpu.SMEM)
MIB = 1024 * 1024


def dot(a, b, ca, cb):
    return lax.dot_general(a, b, (((ca,), (cb,)), ((), ())), preferred_element_type=F32)


def swap(x, axis, bit):
    n = lax.axis_size(axis)
    return lax.ppermute(x, axis, [(i, i ^ bit) for i in range(n)])


def after(x, *others):
    return lax.optimization_barrier((x, others))[0]


def relative(x, index):
    bit = 1
    while bit < x.shape[0]:
        flipped = x.reshape((-1, 2, bit) + x.shape[1:])[:, ::-1].reshape(x.shape)
        x = jnp.where(index & bit != 0, flipped, x)
        bit *= 2
    return x


def spread(x):
    return lax.all_to_all(x, "seq", split_axis=0, concat_axis=0, tiled=True)


def aligned(start, step):
    return pl.multiple_of(start * step, step)


def call(kernel, outs, *args, flops=0, scratch=(), room=60):
    nbytes = sum(x.size * x.dtype.itemsize for x in args + tuple(outs))
    return pl.pallas_call(
        kernel,
        out_shape=list(outs),
        in_specs=[SMEM if x.dtype == jnp.int32 else VMEM for x in args],
        out_specs=[VMEM] * len(outs),
        scratch_shapes=list(scratch),
        compiler_params=pltpu.CompilerParams(vmem_limit_bytes=room * MIB),
        cost_estimate=pl.CostEstimate(flops=flops, bytes_accessed=nbytes, transcendentals=0),
    )(*args)


def shape(dims, dtype=BF16):
    return jax.ShapeDtypeStruct(dims, dtype)


def grad_kernel(part, where, w, tok, cot, near, far, side, tok_far, tok_side, out):
    me = where[0]
    width = cot.shape[1]
    pairs = (
        (cot[...], tok[:, pl.ds(aligned(me, part), part)]),
        (near[:, :width], near[:, width:]),
        (far[...], tok_far[:, :part]),
        (side[...], tok_side[:, part:]),
    )
    for r, (x, t) in enumerate(pairs):
        grad = (dot(x, w[...], 1, 1) * jax.nn.silu(t.astype(F32))).astype(BF16)
        if len(out.shape) == 4:
            offs = out.shape[2]
            for s in range(out.shape[0]):
                out[s, me ^ r] = grad[s * offs : (s + 1) * offs]
        else:
            out[me ^ r] = grad


def rows_of(refs, cols):
    return jnp.concatenate([w[:, cols] for w in refs], axis=0) if len(refs) > 1 else refs[0][:, cols]


def ordered(x, r, y):
    if r < 2:
        return x
    n = x.shape[1] // 3
    a, b, c = x[:, :n], x[:, n : 2 * n], x[:, 2 * n :]
    return jnp.concatenate([jnp.where(y == 0, a, b), jnp.where(y == 0, b, a), c], axis=1)


def gate_kernel(part, piece, tile, where, mix, tok, w0, w1, w2, w3, w4, w5, mon_out, gated_out, t_out, held):
    me, z = where[0], where[1]
    rows, width = tok.shape
    lhs = [mix[:, pl.ds(aligned(me ^ r, part), part)] for r in range(4)]
    weights = ((w0,), (w1,), (w2, w3), (w4, w5))
    for c in range(0, width, tile):
        cols = slice(c, c + tile)
        total = 0.0
        for x, some in zip(lhs, weights):
            total += dot(x, rows_of(some, cols), 1, 0)
        mon = total.astype(BF16)
        mon_out[:, cols] = mon
        wide = tok[:, cols].astype(F32)
        gated = (mon.astype(F32) * jax.nn.silu(wide)).astype(BF16)
        gated_out[:, cols] = gated
        held[cols, :] = gated.T
    if len(t_out.shape) == 3:
        near, outer = t_out.shape[0], t_out.shape[1] // piece
        for i in range(near):
            for rel in range(outer):
                src = (rel ^ z) * near + i
                t_out[i, rel * piece : (rel + 1) * piece, :] = held[pl.ds(aligned(src, piece), piece), :]
    else:
        t_out[...] = held[...]


def carry_kernel(part, where, back, first, term, w0, w1, w2, w3, w4, w5, out):
    me = where[0]
    if len(back.shape) == 4:
        nseq, ndp, offs, _ = back.shape
        parts = [back[:, d].reshape(nseq * offs, part) for d in range(ndp)]
        back = jnp.concatenate(parts, axis=1)
    else:
        back = back[...]
    grad = dot(first[...], back, 0, 0).astype(BF16)
    for r, some in enumerate(((w0,), (w1,), (w2, w3), (w4, w5))):
        cols = pl.ds(aligned(me ^ r, part), part)
        carried = dot(grad, rows_of(some, slice(None)), 1, 1)
        out[:, cols] = (carried + term[:, cols]).astype(BF16)


def last_kernel(part, where, gated, mon, tok, cot, *refs):
    me, y = where[0], where[3]
    mixed, out = refs[-2:]
    weights = (refs[:1], refs[1:2], refs[2:5], refs[5:8])
    for r, some in enumerate(weights):
        cols = pl.ds(aligned(me ^ r, part), part)
        wide = tok[:, cols].astype(F32)
        sigma = jax.nn.sigmoid(wide)
        slope = sigma * (1.0 + wide * (1.0 - sigma))
        grad = ordered(dot(cot[...], rows_of(some, slice(None)), 1, 1), r, y)
        out[:, cols] = grad * mon[:, cols].astype(F32) * slope
    lhs = [ordered(gated[:, pl.ds(aligned(me ^ r, part), part)], r, y) for r in range(4)]
    for c in range(0, mixed.shape[1], part):
        cols = slice(c, c + part)
        total = 0.0
        for x, some in zip(lhs, weights):
            total += dot(x, rows_of(some, cols), 1, 0)
        mixed[:, cols] = total.astype(BF16)


def weight_kernel(tile, starts, where, got, *refs):
    cots, out = refs[: len(starts)], refs[len(starts) :]
    width = out[0].shape[-1]
    here = where[2]
    for c in range(0, width, tile):
        cols = slice(c, c + tile)
        total = 0.0
        for r, (cot, start) in enumerate(zip(cots, starts)):
            total += dot(got[here ^ r], cot[:, c + start : c + start + tile], 1, 0)
        if len(out) == 1:
            out[0][:, cols] = total
            continue
        kept, sent = out
        n, piece, _ = kept.shape
        for i in range(n):
            kept[i, :, cols] = total[2 * i * piece : (2 * i + 1) * piece]
            sent[i, :, cols] = total[(2 * i + 1) * piece : (2 * i + 2) * piece].astype(BF16)


def on_device(tokens, w_in, w_out, first_factor, second_factor, cotangent):
    inputs = tokens[0]
    upstream = cotangent[0]
    first = first_factor[0]
    rows, width = inputs.shape
    nseq = lax.axis_size("seq")
    ndp = lax.axis_size("dp")
    me = lax.axis_index("dp")
    my_s = lax.axis_index("seq")
    flat = my_s * ndp + me
    part = width // ndp
    offs = rows // nseq
    piece = width // (nseq * ndp)
    flops = 2 * rows * width * width

    def columns(x, r):
        return lax.dynamic_slice_in_dim(x, (me ^ r) * part, part, axis=1)

    def unchunk(x):
        return x.transpose(0, 2, 1, 3).reshape(rows, width)

    def halve(x, bit, other=()):
        x = x.reshape(x.shape[0] // 2, 2, piece, width)
        got = swap(x[:, 1].astype(BF16), "seq", 2 * bit)
        got, other = lax.optimization_barrier((got, other))
        return x[:, 0] + got.astype(F32), other

    join = lax.optimization_barrier
    near = 2 * ndp
    outer = nseq // 2
    here = flat % near
    where = jnp.stack([me, flat // near, here, my_s % 2]).astype(jnp.int32)

    split = offs % 16 == 0 and piece % 16 == 0

    some = 2 * (part // 3)
    far_a = swap(w_in[:some], "dp", 2)
    arrived = spread(dot(first, inputs, 1, 0).astype(BF16).reshape(nseq, offs, width))
    pair = swap(upstream, "seq", 1)
    rest = w_in[some:]
    third = part // 3
    outs = lax.dynamic_slice_in_dim(w_out, (my_s % 2) * third, third, axis=0), w_out[some:]
    arrived, far_a, rest, up, outs = join((arrived, far_a, rest, upstream, outs))

    mix = jnp.einsum("sab,bsd->asd", second_factor, arrived, preferred_element_type=F32)
    mix = spread(mix.astype(BF16))
    far_b = swap(rest, "dp", 2)
    side_a = swap(far_a, "dp", 1)
    side_b = swap(far_b, "dp", 1)
    w_near = swap(w_in, "dp", 1)
    cot_near = swap(jnp.concatenate([upstream, columns(inputs, 1)], axis=1), "dp", 1)
    tok_far = jnp.concatenate([columns(inputs, 2), columns(inputs, 3)], axis=1)
    cot_far = swap(up, "dp", 2)
    mix, far_b, side_a, side_b, w_near, cot_near, cot_far, tok_far, outs = join(
        (mix, far_b, side_a, side_b, w_near, cot_near, cot_far, tok_far, outs)
    )

    w_ins = (w_in, w_near, far_a, far_b, side_a, side_b)
    tok_far = swap(tok_far, "dp", 2)
    pair_far = swap(cot_far, "seq", 1)
    cot_side = swap(cot_far, "dp", 1)
    tok_side = swap(tok_far, "dp", 1)
    out_a = swap(outs[0], "dp", 2)
    mix = mix.reshape(rows, width)
    monarch, gated, turned = call(
        functools.partial(gate_kernel, part, piece, part),
        [
            shape((rows, width)),
            shape((rows, width)),
            shape((near, outer * piece, rows) if split else (width, rows)),
        ],
        where,
        mix,
        inputs,
        *w_ins,
        flops=flops,
        scratch=[pltpu.VMEM((width, rows), BF16)],
    )
    if not split:
        turned = relative(turned.reshape(outer, near, piece, rows), flat // near)
        turned = turned.transpose(1, 0, 2, 3).reshape(near, outer * piece, rows)
    groups = [[z * near + i for i in range(near)] for z in range(outer)]
    got = lax.all_to_all(
        turned, ("seq", "dp"), split_axis=0, concat_axis=0, tiled=True, axis_index_groups=groups
    )
    (grads,) = call(
        functools.partial(grad_kernel, part),
        [shape((nseq, ndp, offs, part) if split else (ndp, rows, part))],
        where,
        w_out,
        inputs,
        upstream,
        cot_near,
        cot_far,
        cot_side,
        tok_far,
        tok_side,
        flops=flops,
    )
    if not split:
        grads = grads.reshape(ndp, nseq, offs, part).transpose(1, 0, 2, 3)
    grads = grads.reshape(nseq * ndp, offs, part)
    got, grads, pair, pair_far, outs, out_a = join((got, grads, pair, pair_far, outs, out_a))
    pairs = (pair, swap(pair, "dp", 1), pair_far, swap(pair_far, "dp", 1))
    out_b = swap(out_a, "seq", 1)
    out_c = swap(outs[1], "dp", 2)

    grads = lax.all_to_all(grads, ("seq", "dp"), split_axis=0, concat_axis=0, tiled=True)
    grads = grads.reshape(nseq, ndp, offs, part)
    back = jnp.einsum("sab,ajsc->bjsc", second_factor, grads, preferred_element_type=F32)
    back = back.astype(BF16)
    halves = (outer // 2, piece, width)
    total = call(
        functools.partial(
            weight_kernel, part, (0,) * (2 * ndp)
        ),
        [shape(halves, F32), shape(halves)] if split else [shape((outer * piece, width), F32)],
        where,
        got,
        upstream,
        cot_near,
        cot_far,
        cot_side,
        *pairs,
        flops=flops,
    )
    if not split:
        total = total[0].reshape(outer // 2, 2, piece, width)
        total = (total[:, 0], total[:, 1].astype(BF16))
    kept, sent = total
    sent = swap(sent, "seq", 2)
    sent, back, w_late, out_b, out_c = join((sent, back, w_out, out_b, out_c))
    total = kept + sent.astype(F32)
    bit = 2

    back = spread(back)
    far = (out_a, out_b, out_c)
    w_outs = (w_out, swap(w_late, "dp", 1), *far, *(swap(w, "dp", 1) for w in far))
    mixed, term = call(
        functools.partial(last_kernel, part),
        [shape((rows, width)), shape((rows, width), F32)],
        where,
        gated,
        monarch,
        inputs,
        upstream,
        *w_outs,
        flops=2 * flops,
    )
    if offs % 16 != 0:
        back = unchunk(back)
    (input_grad,) = call(
        functools.partial(carry_kernel, part),
        [shape((rows, width))],
        where,
        back,
        first,
        term,
        *w_ins,
        flops=flops,
    )
    ready = (mixed, input_grad)
    while total.shape[0] > 1:
        total, ready = halve(total, bit, ready)
        bit *= 2
    mixed, input_grad = ready
    weight_grad = total[0] / jnp.sqrt(F32(rows * nseq * ndp))
    return mixed[None], input_grad[None], weight_grad


def solution(mesh):
    placed = (
        P("dp", "seq", None),
        P("dp", None),
        P("dp", None),
        P("seq", None, None),
        P("seq", None, None),
        P("dp", "seq", None),
    )
    return jax.shard_map(
        on_device,
        mesh=mesh,
        in_specs=placed,
        out_specs=(P("dp", "seq", None), P("dp", "seq", None), P(("seq", "dp"), None)),
        check_vma=False,
    )
```

```python
import functools

import jax
import jax.numpy as jnp
from jax import lax
from jax.experimental import pallas as pl
from jax.experimental.pallas import tpu as pltpu
from jax.sharding import PartitionSpec as P

F32 = jnp.float32
BF16 = jnp.bfloat16
VMEM = pl.BlockSpec(memory_space=pltpu.VMEM)
SMEM = pl.BlockSpec(memory_space=pltpu.SMEM)
MIB = 1024 * 1024


def dot(a, b, ca, cb):
    return lax.dot_general(a, b, (((ca,), (cb,)), ((), ())), preferred_element_type=F32)


def swap(x, axis, bit):
    n = lax.axis_size(axis)
    return lax.ppermute(x, axis, [(i, i ^ bit) for i in range(n)])


def after(x, *others):
    return lax.optimization_barrier((x, others))[0]


def relative(x, index):
    bit = 1
    while bit < x.shape[0]:
        flipped = x.reshape((-1, 2, bit) + x.shape[1:])[:, ::-1].reshape(x.shape)
        x = jnp.where(index & bit != 0, flipped, x)
        bit *= 2
    return x


def spread(x):
    return lax.all_to_all(x, "seq", split_axis=0, concat_axis=0, tiled=True)


def aligned(start, step):
    return pl.multiple_of(start * step, step)


def call(kernel, outs, *args, flops=0, scratch=(), room=60):
    nbytes = sum(x.size * x.dtype.itemsize for x in args + tuple(outs))
    return pl.pallas_call(
        kernel,
        out_shape=list(outs),
        in_specs=[SMEM if x.dtype == jnp.int32 else VMEM for x in args],
        out_specs=[VMEM] * len(outs),
        scratch_shapes=list(scratch),
        compiler_params=pltpu.CompilerParams(vmem_limit_bytes=room * MIB),
        cost_estimate=pl.CostEstimate(flops=flops, bytes_accessed=nbytes, transcendentals=0),
    )(*args)


def shape(dims, dtype=BF16):
    return jax.ShapeDtypeStruct(dims, dtype)


def grad_kernel(part, where, w, tok, cot, near, far, side, tok_far, tok_side, out):
    me = where[0]
    width = cot.shape[1]
    pairs = (
        (cot[...], tok[:, pl.ds(aligned(me, part), part)]),
        (near[:, :width], near[:, width:]),
        (far[...], tok_far[:, :part]),
        (side[...], tok_side[:, part:]),
    )
    for r, (x, t) in enumerate(pairs):
        grad = (dot(x, w[...], 1, 1) * jax.nn.silu(t.astype(F32))).astype(BF16)
        if len(out.shape) == 4:
            offs = out.shape[2]
            for s in range(out.shape[0]):
                out[s, me ^ r] = grad[s * offs : (s + 1) * offs]
        else:
            out[me ^ r] = grad


def rows_of(refs, cols):
    return jnp.concatenate([w[:, cols] for w in refs], axis=0) if len(refs) > 1 else refs[0][:, cols]


def ordered(x, r, y):
    if r < 2:
        return x
    n = x.shape[1] // 3
    a, b, c = x[:, :n], x[:, n : 2 * n], x[:, 2 * n :]
    return jnp.concatenate([jnp.where(y == 0, a, b), jnp.where(y == 0, b, a), c], axis=1)


def gate_kernel(part, piece, tile, where, mix, tok, w0, w1, w2, w3, w4, w5, mon_out, gated_out, t_out, held):
    me, z = where[0], where[1]
    rows, width = tok.shape
    lhs = [mix[:, pl.ds(aligned(me ^ r, part), part)] for r in range(4)]
    weights = ((w0,), (w1,), (w2, w3), (w4, w5))
    for c in range(0, width, tile):
        cols = slice(c, c + tile)
        total = 0.0
        for x, some in zip(lhs, weights):
            total += dot(x, rows_of(some, cols), 1, 0)
        mon = total.astype(BF16)
        mon_out[:, cols] = mon
        wide = tok[:, cols].astype(F32)
        gated = (mon.astype(F32) * jax.nn.silu(wide)).astype(BF16)
        gated_out[:, cols] = gated
        held[cols, :] = gated.T
    if len(t_out.shape) == 3:
        near, outer = t_out.shape[0], t_out.shape[1] // piece
        for i in range(near):
            for rel in range(outer):
                src = (rel ^ z) * near + i
                t_out[i, rel * piece : (rel + 1) * piece, :] = held[pl.ds(aligned(src, piece), piece), :]
    else:
        t_out[...] = held[...]


def carry_kernel(part, where, back, first, term, w0, w1, w2, w3, w4, w5, out):
    me = where[0]
    if len(back.shape) == 4:
        nseq, ndp, offs, _ = back.shape
        parts = [back[:, d].reshape(nseq * offs, part) for d in range(ndp)]
        back = jnp.concatenate(parts, axis=1)
    else:
        back = back[...]
    grad = dot(first[...], back, 0, 0).astype(BF16)
    for r, some in enumerate(((w0,), (w1,), (w2, w3), (w4, w5))):
        cols = pl.ds(aligned(me ^ r, part), part)
        carried = dot(grad, rows_of(some, slice(None)), 1, 1)
        out[:, cols] = (carried + term[:, cols]).astype(BF16)


def last_kernel(part, where, gated, mon, tok, cot, *refs):
    me, y = where[0], where[3]
    mixed, out = refs[-2:]
    weights = (refs[:1], refs[1:2], refs[2:5], refs[5:8])
    for r, some in enumerate(weights):
        cols = pl.ds(aligned(me ^ r, part), part)
        wide = tok[:, cols].astype(F32)
        sigma = jax.nn.sigmoid(wide)
        slope = sigma * (1.0 + wide * (1.0 - sigma))
        grad = ordered(dot(cot[...], rows_of(some, slice(None)), 1, 1), r, y)
        out[:, cols] = grad * mon[:, cols].astype(F32) * slope
    lhs = [ordered(gated[:, pl.ds(aligned(me ^ r, part), part)], r, y) for r in range(4)]
    for c in range(0, mixed.shape[1], part):
        cols = slice(c, c + part)
        total = 0.0
        for x, some in zip(lhs, weights):
            total += dot(x, rows_of(some, cols), 1, 0)
        mixed[:, cols] = total.astype(BF16)


def weight_kernel(tile, starts, where, got, *refs):
    cots, out = refs[: len(starts)], refs[len(starts) :]
    width = out[0].shape[-1]
    here = where[2]
    for c in range(0, width, tile):
        cols = slice(c, c + tile)
        total = 0.0
        for r, (cot, start) in enumerate(zip(cots, starts)):
            total += dot(got[here ^ r], cot[:, c + start : c + start + tile], 1, 0)
        if len(out) == 1:
            out[0][:, cols] = total
            continue
        kept, sent = out
        n, piece, _ = kept.shape
        for i in range(n):
            kept[i, :, cols] = total[2 * i * piece : (2 * i + 1) * piece]
            sent[i, :, cols] = total[(2 * i + 1) * piece : (2 * i + 2) * piece].astype(BF16)


def on_device(tokens, w_in, w_out, first_factor, second_factor, cotangent):
    inputs = tokens[0]
    upstream = cotangent[0]
    first = first_factor[0]
    rows, width = inputs.shape
    nseq = lax.axis_size("seq")
    ndp = lax.axis_size("dp")
    me = lax.axis_index("dp")
    my_s = lax.axis_index("seq")
    flat = my_s * ndp + me
    part = width // ndp
    offs = rows // nseq
    piece = width // (nseq * ndp)
    flops = 2 * rows * width * width

    def columns(x, r):
        return lax.dynamic_slice_in_dim(x, (me ^ r) * part, part, axis=1)

    def unchunk(x):
        return x.transpose(0, 2, 1, 3).reshape(rows, width)

    def halve(x, bit, other=()):
        x = x.reshape(x.shape[0] // 2, 2, piece, width)
        got = swap(x[:, 1].astype(BF16), "seq", 2 * bit)
        got, other = lax.optimization_barrier((got, other))
        return x[:, 0] + got.astype(F32), other

    join = lax.optimization_barrier
    near = 2 * ndp
    outer = nseq // 2
    here = flat % near
    where = jnp.stack([me, flat // near, here, my_s % 2]).astype(jnp.int32)

    split = offs % 16 == 0 and piece % 16 == 0

    some = 2 * (part // 3)
    far_a = swap(w_in[:some], "dp", 2)
    arrived = spread(dot(first, inputs, 1, 0).astype(BF16).reshape(nseq, offs, width))
    pair = swap(upstream, "seq", 1)
    rest = w_in[some:]
    third = part // 3
    outs = lax.dynamic_slice_in_dim(w_out, (my_s % 2) * third, third, axis=0), w_out[some:]
    arrived, far_a, rest, up, outs = join((arrived, far_a, rest, upstream, outs))

    mix = jnp.einsum("sab,bsd->asd", second_factor, arrived, preferred_element_type=F32)
    mix = spread(mix.astype(BF16))
    far_b = swap(rest, "dp", 2)
    side_a = swap(far_a, "dp", 1)
    side_b = swap(far_b, "dp", 1)
    w_near = swap(w_in, "dp", 1)
    cot_near = swap(jnp.concatenate([upstream, columns(inputs, 1)], axis=1), "dp", 1)
    tok_far = jnp.concatenate([columns(inputs, 2), columns(inputs, 3)], axis=1)
    cot_far = swap(up, "dp", 2)
    mix, far_b, side_a, side_b, w_near, cot_near, cot_far, tok_far, outs = join(
        (mix, far_b, side_a, side_b, w_near, cot_near, cot_far, tok_far, outs)
    )

    w_ins = (w_in, w_near, far_a, far_b, side_a, side_b)
    tok_far = swap(tok_far, "dp", 2)
    pair_far = swap(cot_far, "seq", 1)
    cot_side = swap(cot_far, "dp", 1)
    tok_side = swap(tok_far, "dp", 1)
    out_a = swap(outs[0], "dp", 2)
    mix = mix.reshape(rows, width)
    monarch, gated, turned = call(
        functools.partial(gate_kernel, part, piece, part),
        [
            shape((rows, width)),
            shape((rows, width)),
            shape((near, outer * piece, rows) if split else (width, rows)),
        ],
        where,
        mix,
        inputs,
        *w_ins,
        flops=flops,
        scratch=[pltpu.VMEM((width, rows), BF16)],
    )
    if not split:
        turned = relative(turned.reshape(outer, near, piece, rows), flat // near)
        turned = turned.transpose(1, 0, 2, 3).reshape(near, outer * piece, rows)
    groups = [[z * near + i for i in range(near)] for z in range(outer)]
    got = lax.all_to_all(
        turned, ("seq", "dp"), split_axis=0, concat_axis=0, tiled=True, axis_index_groups=groups
    )
    (grads,) = call(
        functools.partial(grad_kernel, part),
        [shape((nseq, ndp, offs, part) if split else (ndp, rows, part))],
        where,
        w_out,
        inputs,
        upstream,
        cot_near,
        cot_far,
        cot_side,
        tok_far,
        tok_side,
        flops=flops,
    )
    if not split:
        grads = grads.reshape(ndp, nseq, offs, part).transpose(1, 0, 2, 3)
    grads = grads.reshape(nseq * ndp, offs, part)
    got, grads, pair, pair_far, outs, out_a = join((got, grads, pair, pair_far, outs, out_a))
    pairs = (pair, swap(pair, "dp", 1), pair_far, swap(pair_far, "dp", 1))
    out_b = swap(out_a, "seq", 1)
    out_c = swap(outs[1], "dp", 2)

    grads = lax.all_to_all(grads, ("seq", "dp"), split_axis=0, concat_axis=0, tiled=True)
    grads = grads.reshape(nseq, ndp, offs, part)
    back = jnp.einsum("sab,ajsc->bjsc", second_factor, grads, preferred_element_type=F32)
    back = back.astype(BF16)
    halves = (outer // 2, piece, width)
    total = call(
        functools.partial(
            weight_kernel, part, (0,) * (2 * ndp)
        ),
        [shape(halves, F32), shape(halves)] if split else [shape((outer * piece, width), F32)],
        where,
        got,
        upstream,
        cot_near,
        cot_far,
        cot_side,
        *pairs,
        flops=flops,
    )
    if not split:
        total = total[0].reshape(outer // 2, 2, piece, width)
        total = (total[:, 0], total[:, 1].astype(BF16))
    kept, sent = total
    sent = swap(sent, "seq", 2)
    sent, back = join((sent, back))
    w_late = w_out
    total = kept + sent.astype(F32)
    bit = 2

    back = spread(back)
    far = (out_a, out_b, out_c)
    w_outs = (w_out, swap(w_late, "dp", 1), *far, *(swap(w, "dp", 1) for w in far))
    mixed, term = call(
        functools.partial(last_kernel, part),
        [shape((rows, width)), shape((rows, width), F32)],
        where,
        gated,
        monarch,
        inputs,
        upstream,
        *w_outs,
        flops=2 * flops,
    )
    if offs % 16 != 0:
        back = unchunk(back)
    (input_grad,) = call(
        functools.partial(carry_kernel, part),
        [shape((rows, width))],
        where,
        back,
        first,
        term,
        *w_ins,
        flops=flops,
        room=40,
    )
    ready = (mixed, input_grad)
    while total.shape[0] > 1:
        total, ready = halve(total, bit, ready)
        bit *= 2
    mixed, input_grad = ready
    weight_grad = total[0] / jnp.sqrt(F32(rows * nseq * ndp))
    return mixed[None], input_grad[None], weight_grad


def solution(mesh):
    placed = (
        P("dp", "seq", None),
        P("dp", None),
        P("dp", None),
        P("seq", None, None),
        P("seq", None, None),
        P("dp", "seq", None),
    )
    return jax.shard_map(
        on_device,
        mesh=mesh,
        in_specs=placed,
        out_specs=(P("dp", "seq", None), P("dp", "seq", None), P(("seq", "dp"), None)),
        check_vma=False,
    )
```

```python
import functools

import jax
import jax.numpy as jnp
from jax import lax
from jax.experimental import pallas as pl
from jax.experimental.pallas import tpu as pltpu
from jax.sharding import PartitionSpec as P

F32 = jnp.float32
BF16 = jnp.bfloat16
VMEM = pl.BlockSpec(memory_space=pltpu.VMEM)
SMEM = pl.BlockSpec(memory_space=pltpu.SMEM)
MIB = 1024 * 1024


def dot(a, b, ca, cb):
    return lax.dot_general(a, b, (((ca,), (cb,)), ((), ())), preferred_element_type=F32)


def swap(x, axis, bit):
    n = lax.axis_size(axis)
    return lax.ppermute(x, axis, [(i, i ^ bit) for i in range(n)])


def after(x, *others):
    return lax.optimization_barrier((x, others))[0]


def relative(x, index):
    bit = 1
    while bit < x.shape[0]:
        flipped = x.reshape((-1, 2, bit) + x.shape[1:])[:, ::-1].reshape(x.shape)
        x = jnp.where(index & bit != 0, flipped, x)
        bit *= 2
    return x


def spread(x):
    return lax.all_to_all(x, "seq", split_axis=0, concat_axis=0, tiled=True)


def aligned(start, step):
    return pl.multiple_of(start * step, step)


def call(kernel, outs, *args, flops=0, scratch=(), room=60):
    nbytes = sum(x.size * x.dtype.itemsize for x in args + tuple(outs))
    return pl.pallas_call(
        kernel,
        out_shape=list(outs),
        in_specs=[SMEM if x.dtype == jnp.int32 else VMEM for x in args],
        out_specs=[VMEM] * len(outs),
        scratch_shapes=list(scratch),
        compiler_params=pltpu.CompilerParams(vmem_limit_bytes=room * MIB),
        cost_estimate=pl.CostEstimate(flops=flops, bytes_accessed=nbytes, transcendentals=0),
    )(*args)


def shape(dims, dtype=BF16):
    return jax.ShapeDtypeStruct(dims, dtype)


def grad_kernel(part, where, w, tok, cot, near, far, side, tok_far, tok_side, out):
    me = where[0]
    width = cot.shape[1]
    pairs = (
        (cot[...], tok[:, pl.ds(aligned(me, part), part)]),
        (near[:, :width], near[:, width:]),
        (far[...], tok_far[:, :part]),
        (side[...], tok_side[:, part:]),
    )
    for r, (x, t) in enumerate(pairs):
        grad = (dot(x, w[...], 1, 1) * jax.nn.silu(t.astype(F32))).astype(BF16)
        if len(out.shape) == 4:
            offs = out.shape[2]
            for s in range(out.shape[0]):
                out[s, me ^ r] = grad[s * offs : (s + 1) * offs]
        else:
            out[me ^ r] = grad


def rows_of(refs, cols):
    return jnp.concatenate([w[:, cols] for w in refs], axis=0) if len(refs) > 1 else refs[0][:, cols]


def ordered(x, r, y):
    if r < 2:
        return x
    n = x.shape[1] // 3
    a, b, c = x[:, :n], x[:, n : 2 * n], x[:, 2 * n :]
    return jnp.concatenate([jnp.where(y == 0, a, b), jnp.where(y == 0, b, a), c], axis=1)


def gate_kernel(part, piece, tile, where, mix, tok, w0, w1, w2, w3, w4, w5, mon_out, gated_out, t_out, held):
    me, z = where[0], where[1]
    rows, width = tok.shape
    lhs = [mix[:, pl.ds(aligned(me ^ r, part), part)] for r in range(4)]
    weights = ((w0,), (w1,), (w2, w3), (w4, w5))
    for c in range(0, width, tile):
        cols = slice(c, c + tile)
        total = 0.0
        for x, some in zip(lhs, weights):
            total += dot(x, rows_of(some, cols), 1, 0)
        mon = total.astype(BF16)
        mon_out[:, cols] = mon
        wide = tok[:, cols].astype(F32)
        gated = (mon.astype(F32) * jax.nn.silu(wide)).astype(BF16)
        gated_out[:, cols] = gated
        held[cols, :] = gated.T
    if len(t_out.shape) == 3:
        near, outer = t_out.shape[0], t_out.shape[1] // piece
        for i in range(near):
            for rel in range(outer):
                src = (rel ^ z) * near + i
                t_out[i, rel * piece : (rel + 1) * piece, :] = held[pl.ds(aligned(src, piece), piece), :]
    else:
        t_out[...] = held[...]


def carry_kernel(part, where, back, first, term, w0, w1, w2, w3, w4, w5, out):
    me = where[0]
    if len(back.shape) == 4:
        nseq, ndp, offs, _ = back.shape
        parts = [back[:, d].reshape(nseq * offs, part) for d in range(ndp)]
        back = jnp.concatenate(parts, axis=1)
    else:
        back = back[...]
    grad = dot(first[...], back, 0, 0).astype(BF16)
    for r, some in enumerate(((w0,), (w1,), (w2, w3), (w4, w5))):
        cols = pl.ds(aligned(me ^ r, part), part)
        carried = dot(grad, rows_of(some, slice(None)), 1, 1)
        out[:, cols] = (carried + term[:, cols]).astype(BF16)


def last_kernel(part, where, gated, mon, tok, cot, *refs):
    me, y = where[0], where[3]
    mixed, out = refs[-2:]
    weights = (refs[:1], refs[1:2], refs[2:5], refs[5:8])
    for r, some in enumerate(weights):
        cols = pl.ds(aligned(me ^ r, part), part)
        wide = tok[:, cols].astype(F32)
        sigma = jax.nn.sigmoid(wide)
        slope = sigma * (1.0 + wide * (1.0 - sigma))
        grad = ordered(dot(cot[...], rows_of(some, slice(None)), 1, 1), r, y)
        out[:, cols] = grad * mon[:, cols].astype(F32) * slope
    lhs = [ordered(gated[:, pl.ds(aligned(me ^ r, part), part)], r, y) for r in range(4)]
    for c in range(0, mixed.shape[1], part):
        cols = slice(c, c + part)
        total = 0.0
        for x, some in zip(lhs, weights):
            total += dot(x, rows_of(some, cols), 1, 0)
        mixed[:, cols] = total.astype(BF16)


def weight_kernel(tile, starts, where, got, *refs):
    cots, out = refs[: len(starts)], refs[len(starts) :]
    width = out[0].shape[-1]
    here = where[2]
    for c in range(0, width, tile):
        cols = slice(c, c + tile)
        total = 0.0
        for r, (cot, start) in enumerate(zip(cots, starts)):
            total += dot(got[here ^ r], cot[:, c + start : c + start + tile], 1, 0)
        if len(out) == 1:
            out[0][:, cols] = total
            continue
        kept, sent = out
        n, piece, _ = kept.shape
        for i in range(n):
            kept[i, :, cols] = total[2 * i * piece : (2 * i + 1) * piece]
            sent[i, :, cols] = total[(2 * i + 1) * piece : (2 * i + 2) * piece].astype(BF16)


def on_device(tokens, w_in, w_out, first_factor, second_factor, cotangent):
    inputs = tokens[0]
    upstream = cotangent[0]
    first = first_factor[0]
    rows, width = inputs.shape
    nseq = lax.axis_size("seq")
    ndp = lax.axis_size("dp")
    me = lax.axis_index("dp")
    my_s = lax.axis_index("seq")
    flat = my_s * ndp + me
    part = width // ndp
    offs = rows // nseq
    piece = width // (nseq * ndp)
    flops = 2 * rows * width * width

    def columns(x, r):
        return lax.dynamic_slice_in_dim(x, (me ^ r) * part, part, axis=1)

    def unchunk(x):
        return x.transpose(0, 2, 1, 3).reshape(rows, width)

    def halve(x, bit, other=()):
        x = x.reshape(x.shape[0] // 2, 2, piece, width)
        got = swap(x[:, 1].astype(BF16), "seq", 2 * bit)
        got, other = lax.optimization_barrier((got, other))
        return x[:, 0] + got.astype(F32), other

    join = lax.optimization_barrier
    near = 2 * ndp
    outer = nseq // 2
    here = flat % near
    where = jnp.stack([me, flat // near, here, my_s % 2]).astype(jnp.int32)

    split = offs % 16 == 0 and piece % 16 == 0

    some = 2 * (part // 3)
    far_a = swap(w_in[:some], "dp", 2)
    arrived = spread(dot(first, inputs, 1, 0).astype(BF16).reshape(nseq, offs, width))
    pair = swap(upstream, "seq", 1)
    rest = w_in[some:]
    third = part // 3
    outs = lax.dynamic_slice_in_dim(w_out, (my_s % 2) * third, third, axis=0), w_out[some:]
    arrived, far_a, rest, up, outs = join((arrived, far_a, rest, upstream, outs))

    mix = jnp.einsum("sab,bsd->asd", second_factor, arrived, preferred_element_type=F32)
    mix = spread(mix.astype(BF16))
    far_b = swap(rest, "dp", 2)
    side_a = swap(far_a, "dp", 1)
    side_b = swap(far_b, "dp", 1)
    w_near = swap(w_in, "dp", 1)
    cot_near = swap(jnp.concatenate([upstream, columns(inputs, 1)], axis=1), "dp", 1)
    tok_far = jnp.concatenate([columns(inputs, 2), columns(inputs, 3)], axis=1)
    cot_far = swap(up, "dp", 2)
    cot_side = swap(cot_far, "dp", 1)
    mix, far_b, side_a, side_b, w_near, cot_near, cot_far, cot_side, tok_far, outs, pair = join(
        (mix, far_b, side_a, side_b, w_near, cot_near, cot_far, cot_side, tok_far, outs, pair)
    )

    w_ins = (w_in, w_near, far_a, far_b, side_a, side_b)
    tok_far = swap(tok_far, "dp", 2)
    pair_far = swap(cot_far, "seq", 1)
    tok_side = swap(tok_far, "dp", 1)
    out_a = swap(outs[0], "dp", 2)
    mix = mix.reshape(rows, width)
    monarch, gated, turned = call(
        functools.partial(gate_kernel, part, piece, part),
        [
            shape((rows, width)),
            shape((rows, width)),
            shape((near, outer * piece, rows) if split else (width, rows)),
        ],
        where,
        mix,
        inputs,
        *w_ins,
        flops=flops,
        scratch=[pltpu.VMEM((width, rows), BF16)],
    )
    if not split:
        turned = relative(turned.reshape(outer, near, piece, rows), flat // near)
        turned = turned.transpose(1, 0, 2, 3).reshape(near, outer * piece, rows)
    groups = [[z * near + i for i in range(near)] for z in range(outer)]
    got = lax.all_to_all(
        turned, ("seq", "dp"), split_axis=0, concat_axis=0, tiled=True, axis_index_groups=groups
    )
    (grads,) = call(
        functools.partial(grad_kernel, part),
        [shape((nseq, ndp, offs, part) if split else (ndp, rows, part))],
        where,
        w_out,
        inputs,
        upstream,
        cot_near,
        cot_far,
        cot_side,
        tok_far,
        tok_side,
        flops=flops,
    )
    if not split:
        grads = grads.reshape(ndp, nseq, offs, part).transpose(1, 0, 2, 3)
    grads = grads.reshape(nseq * ndp, offs, part)
    got, grads, pair, pair_far, outs, out_a = join((got, grads, pair, pair_far, outs, out_a))
    pairs = (pair, swap(pair, "dp", 1), pair_far, swap(pair_far, "dp", 1))
    out_b = swap(out_a, "seq", 1)
    out_c = swap(outs[1], "dp", 2)

    grads = lax.all_to_all(grads, ("seq", "dp"), split_axis=0, concat_axis=0, tiled=True)
    grads = grads.reshape(nseq, ndp, offs, part)
    back = jnp.einsum("sab,ajsc->bjsc", second_factor, grads, preferred_element_type=F32)
    back = back.astype(BF16)
    halves = (outer // 2, piece, width)
    total = call(
        functools.partial(
            weight_kernel, part, (0,) * (2 * ndp)
        ),
        [shape(halves, F32), shape(halves)] if split else [shape((outer * piece, width), F32)],
        where,
        got,
        upstream,
        cot_near,
        cot_far,
        cot_side,
        *pairs,
        flops=flops,
    )
    if not split:
        total = total[0].reshape(outer // 2, 2, piece, width)
        total = (total[:, 0], total[:, 1].astype(BF16))
    kept, sent = total
    sent = swap(sent, "seq", 2)
    sent, back = join((sent, back))
    w_late = w_out
    total = kept + sent.astype(F32)
    bit = 2

    back = spread(back)
    far = (out_a, out_b, out_c)
    w_outs = (w_out, swap(w_late, "dp", 1), *far, *(swap(w, "dp", 1) for w in far))
    mixed, term = call(
        functools.partial(last_kernel, part),
        [shape((rows, width)), shape((rows, width), F32)],
        where,
        gated,
        monarch,
        inputs,
        upstream,
        *w_outs,
        flops=2 * flops,
    )
    if offs % 16 != 0:
        back = unchunk(back)
    (input_grad,) = call(
        functools.partial(carry_kernel, part),
        [shape((rows, width))],
        where,
        back,
        first,
        term,
        *w_ins,
        flops=flops,
        room=40,
    )
    ready = (mixed, input_grad)
    while total.shape[0] > 1:
        total, ready = halve(total, bit, ready)
        bit *= 2
    mixed, input_grad = ready
    weight_grad = total[0] / jnp.sqrt(F32(rows * nseq * ndp))
    return mixed[None], input_grad[None], weight_grad


def solution(mesh):
    placed = (
        P("dp", "seq", None),
        P("dp", None),
        P("dp", None),
        P("seq", None, None),
        P("seq", None, None),
        P("dp", "seq", None),
    )
    return jax.shard_map(
        on_device,
        mesh=mesh,
        in_specs=placed,
        out_specs=(P("dp", "seq", None), P("dp", "seq", None), P(("seq", "dp"), None)),
        check_vma=False,
    )
```

```python
import functools

import jax
import jax.numpy as jnp
from jax import lax
from jax.experimental import pallas as pl
from jax.experimental.pallas import tpu as pltpu
from jax.sharding import PartitionSpec as P

F32 = jnp.float32
BF16 = jnp.bfloat16
VMEM = pl.BlockSpec(memory_space=pltpu.VMEM)
SMEM = pl.BlockSpec(memory_space=pltpu.SMEM)
MIB = 1024 * 1024


def dot(a, b, ca, cb):
    return lax.dot_general(a, b, (((ca,), (cb,)), ((), ())), preferred_element_type=F32)


def swap(x, axis, bit):
    n = lax.axis_size(axis)
    return lax.ppermute(x, axis, [(i, i ^ bit) for i in range(n)])


def after(x, *others):
    return lax.optimization_barrier((x, others))[0]


def relative(x, index):
    bit = 1
    while bit < x.shape[0]:
        flipped = x.reshape((-1, 2, bit) + x.shape[1:])[:, ::-1].reshape(x.shape)
        x = jnp.where(index & bit != 0, flipped, x)
        bit *= 2
    return x


def spread(x):
    return lax.all_to_all(x, "seq", split_axis=0, concat_axis=0, tiled=True)


def aligned(start, step):
    return pl.multiple_of(start * step, step)


def call(kernel, outs, *args, flops=0, scratch=(), room=60):
    nbytes = sum(x.size * x.dtype.itemsize for x in args + tuple(outs))
    return pl.pallas_call(
        kernel,
        out_shape=list(outs),
        in_specs=[SMEM if x.dtype == jnp.int32 else VMEM for x in args],
        out_specs=[VMEM] * len(outs),
        scratch_shapes=list(scratch),
        compiler_params=pltpu.CompilerParams(vmem_limit_bytes=room * MIB),
        cost_estimate=pl.CostEstimate(flops=flops, bytes_accessed=nbytes, transcendentals=0),
    )(*args)


def shape(dims, dtype=BF16):
    return jax.ShapeDtypeStruct(dims, dtype)


def grad_kernel(part, where, w, tok, cot, near, far, side, tok_far, tok_side, out):
    me = where[0]
    width = cot.shape[1]
    pairs = (
        (cot[...], tok[:, pl.ds(aligned(me, part), part)]),
        (near[:, :width], near[:, width:]),
        (far[...], tok_far[:, :part]),
        (side[...], tok_side[:, part:]),
    )
    for r, (x, t) in enumerate(pairs):
        grad = (dot(x, w[...], 1, 1) * jax.nn.silu(t.astype(F32))).astype(BF16)
        if len(out.shape) == 4:
            offs = out.shape[2]
            for s in range(out.shape[0]):
                out[s, me ^ r] = grad[s * offs : (s + 1) * offs]
        else:
            out[me ^ r] = grad


def rows_of(refs, cols):
    return jnp.concatenate([w[:, cols] for w in refs], axis=0) if len(refs) > 1 else refs[0][:, cols]


def ordered(x, r, y):
    if r < 2:
        return x
    n = x.shape[1] // 3
    a, b, c = x[:, :n], x[:, n : 2 * n], x[:, 2 * n :]
    return jnp.concatenate([jnp.where(y == 0, a, b), jnp.where(y == 0, b, a), c], axis=1)


def gate_kernel(part, piece, tile, where, mix, tok, w0, w1, w2, w3, w4, w5, mon_out, gated_out, t_out, held):
    me, z = where[0], where[1]
    rows, width = tok.shape
    lhs = [mix[:, pl.ds(aligned(me ^ r, part), part)] for r in range(4)]
    weights = ((w0,), (w1,), (w2, w3), (w4, w5))
    for c in range(0, width, tile):
        cols = slice(c, c + tile)
        total = 0.0
        for x, some in zip(lhs, weights):
            total += dot(x, rows_of(some, cols), 1, 0)
        mon = total.astype(BF16)
        mon_out[:, cols] = mon
        wide = tok[:, cols].astype(F32)
        gated = (mon.astype(F32) * jax.nn.silu(wide)).astype(BF16)
        gated_out[:, cols] = gated
        held[cols, :] = gated.T
    if len(t_out.shape) == 3:
        near, outer = t_out.shape[0], t_out.shape[1] // piece
        for i in range(near):
            for rel in range(outer):
                src = (rel ^ z) * near + i
                t_out[i, rel * piece : (rel + 1) * piece, :] = held[pl.ds(aligned(src, piece), piece), :]
    else:
        t_out[...] = held[...]


def carry_kernel(part, where, back, first, term, w0, w1, w2, w3, w4, w5, out):
    me = where[0]
    if len(back.shape) == 4:
        nseq, ndp, offs, _ = back.shape
        parts = [back[:, d].reshape(nseq * offs, part) for d in range(ndp)]
        back = jnp.concatenate(parts, axis=1)
    else:
        back = back[...]
    grad = dot(first[...], back, 0, 0).astype(BF16)
    for r, some in enumerate(((w0,), (w1,), (w2, w3), (w4, w5))):
        cols = pl.ds(aligned(me ^ r, part), part)
        carried = dot(grad, rows_of(some, slice(None)), 1, 1)
        out[:, cols] = (carried + term[:, cols]).astype(BF16)


def last_kernel(part, where, gated, mon, tok, cot, *refs):
    me, y = where[0], where[3]
    mixed, out = refs[-2:]
    weights = (refs[:1], refs[1:2], refs[2:5], refs[5:8])
    for r, some in enumerate(weights):
        cols = pl.ds(aligned(me ^ r, part), part)
        wide = tok[:, cols].astype(F32)
        sigma = jax.nn.sigmoid(wide)
        slope = sigma * (1.0 + wide * (1.0 - sigma))
        grad = ordered(dot(cot[...], rows_of(some, slice(None)), 1, 1), r, y)
        out[:, cols] = grad * mon[:, cols].astype(F32) * slope
    lhs = [ordered(gated[:, pl.ds(aligned(me ^ r, part), part)], r, y) for r in range(4)]
    for c in range(0, mixed.shape[1], part):
        cols = slice(c, c + part)
        total = 0.0
        for x, some in zip(lhs, weights):
            total += dot(x, rows_of(some, cols), 1, 0)
        mixed[:, cols] = total.astype(BF16)


def weight_kernel(tile, starts, where, got, *refs):
    cots, out = refs[: len(starts)], refs[len(starts) :]
    width = out[0].shape[-1]
    here = where[2]
    for c in range(0, width, tile):
        cols = slice(c, c + tile)
        total = 0.0
        for r, (cot, start) in enumerate(zip(cots, starts)):
            total += dot(got[here ^ r], cot[:, c + start : c + start + tile], 1, 0)
        if len(out) == 1:
            out[0][:, cols] = total
            continue
        kept, sent = out
        n, piece, _ = kept.shape
        for i in range(n):
            kept[i, :, cols] = total[2 * i * piece : (2 * i + 1) * piece]
            sent[i, :, cols] = total[(2 * i + 1) * piece : (2 * i + 2) * piece].astype(BF16)


def on_device(tokens, w_in, w_out, first_factor, second_factor, cotangent):
    inputs = tokens[0]
    upstream = cotangent[0]
    first = first_factor[0]
    rows, width = inputs.shape
    nseq = lax.axis_size("seq")
    ndp = lax.axis_size("dp")
    me = lax.axis_index("dp")
    my_s = lax.axis_index("seq")
    flat = my_s * ndp + me
    part = width // ndp
    offs = rows // nseq
    piece = width // (nseq * ndp)
    flops = 2 * rows * width * width

    def columns(x, r):
        return lax.dynamic_slice_in_dim(x, (me ^ r) * part, part, axis=1)

    def unchunk(x):
        return x.transpose(0, 2, 1, 3).reshape(rows, width)

    def halve(x, bit, other=()):
        x = x.reshape(x.shape[0] // 2, 2, piece, width)
        got = swap(x[:, 1].astype(BF16), "seq", 2 * bit)
        got, other = lax.optimization_barrier((got, other))
        return x[:, 0] + got.astype(F32), other

    join = lax.optimization_barrier
    near = 2 * ndp
    outer = nseq // 2
    here = flat % near
    where = jnp.stack([me, flat // near, here, my_s % 2]).astype(jnp.int32)

    split = offs % 16 == 0 and piece % 16 == 0

    some = 2 * (part // 3)
    far_a = swap(w_in[:some], "dp", 2)
    arrived = spread(dot(first, inputs, 1, 0).astype(BF16).reshape(nseq, offs, width))
    pair = swap(upstream, "seq", 1)
    rest = w_in[some:]
    third = part // 3
    outs = lax.dynamic_slice_in_dim(w_out, (my_s % 2) * third, third, axis=0), w_out[some:]
    arrived, far_a, rest, up, outs = join((arrived, far_a, rest, upstream, outs))

    mix = jnp.einsum("sab,bsd->asd", second_factor, arrived, preferred_element_type=F32)
    mix = spread(mix.astype(BF16))
    far_b = swap(rest, "dp", 2)
    side_a = swap(far_a, "dp", 1)
    side_b = swap(far_b, "dp", 1)
    w_near = swap(w_in, "dp", 1)
    cot_near = swap(jnp.concatenate([upstream, columns(inputs, 1)], axis=1), "dp", 1)
    tok_far = jnp.concatenate([columns(inputs, 2), columns(inputs, 3)], axis=1)
    cot_far = swap(up, "dp", 2)
    cot_side = swap(cot_far, "dp", 1)
    mix, far_b, side_a, side_b, w_near, cot_near, cot_far, cot_side, tok_far, outs, pair = join(
        (mix, far_b, side_a, side_b, w_near, cot_near, cot_far, cot_side, tok_far, outs, pair)
    )

    w_ins = (w_in, w_near, far_a, far_b, side_a, side_b)
    tok_far = swap(tok_far, "dp", 2)
    pair_far = swap(cot_far, "seq", 1)
    tok_side = swap(tok_far, "dp", 1)
    out_a = swap(outs[0], "dp", 2)
    mix = mix.reshape(rows, width)
    monarch, gated, turned = call(
        functools.partial(gate_kernel, part, piece, part),
        [
            shape((rows, width)),
            shape((rows, width)),
            shape((near, outer * piece, rows) if split else (width, rows)),
        ],
        where,
        mix,
        inputs,
        *w_ins,
        flops=flops,
        scratch=[pltpu.VMEM((width, rows), BF16)],
    )
    if not split:
        turned = relative(turned.reshape(outer, near, piece, rows), flat // near)
        turned = turned.transpose(1, 0, 2, 3).reshape(near, outer * piece, rows)
    groups = [[z * near + i for i in range(near)] for z in range(outer)]
    got = lax.all_to_all(
        turned, ("seq", "dp"), split_axis=0, concat_axis=0, tiled=True, axis_index_groups=groups
    )
    (grads,) = call(
        functools.partial(grad_kernel, part),
        [shape((nseq, ndp, offs, part) if split else (ndp, rows, part))],
        where,
        w_out,
        inputs,
        upstream,
        cot_near,
        cot_far,
        cot_side,
        tok_far,
        tok_side,
        flops=flops,
        room=40,
    )
    if not split:
        grads = grads.reshape(ndp, nseq, offs, part).transpose(1, 0, 2, 3)
    grads = grads.reshape(nseq * ndp, offs, part)
    got, grads, pair, pair_far, outs, out_a = join((got, grads, pair, pair_far, outs, out_a))
    pairs = (pair, swap(pair, "dp", 1), pair_far, swap(pair_far, "dp", 1))
    out_b = swap(out_a, "seq", 1)
    out_c = swap(outs[1], "dp", 2)

    grads = lax.all_to_all(grads, ("seq", "dp"), split_axis=0, concat_axis=0, tiled=True)
    grads = grads.reshape(nseq, ndp, offs, part)
    back = jnp.einsum("sab,ajsc->bjsc", second_factor, grads, preferred_element_type=F32)
    back = back.astype(BF16)
    halves = (outer // 2, piece, width)
    total = call(
        functools.partial(
            weight_kernel, part, (0,) * (2 * ndp)
        ),
        [shape(halves, F32), shape(halves)] if split else [shape((outer * piece, width), F32)],
        where,
        got,
        upstream,
        cot_near,
        cot_far,
        cot_side,
        *pairs,
        flops=flops,
    )
    if not split:
        total = total[0].reshape(outer // 2, 2, piece, width)
        total = (total[:, 0], total[:, 1].astype(BF16))
    kept, sent = total
    sent = swap(sent, "seq", 2)
    sent, back = join((sent, back))
    w_late = w_out
    total = kept + sent.astype(F32)
    bit = 2

    back = spread(back)
    far = (out_a, out_b, out_c)
    w_outs = (w_out, swap(w_late, "dp", 1), *far, *(swap(w, "dp", 1) for w in far))
    mixed, term = call(
        functools.partial(last_kernel, part),
        [shape((rows, width)), shape((rows, width), F32)],
        where,
        gated,
        monarch,
        inputs,
        upstream,
        *w_outs,
        flops=2 * flops,
    )
    if offs % 16 != 0:
        back = unchunk(back)
    (input_grad,) = call(
        functools.partial(carry_kernel, part),
        [shape((rows, width))],
        where,
        back,
        first,
        term,
        *w_ins,
        flops=flops,
        room=40,
    )
    ready = (mixed, input_grad)
    while total.shape[0] > 1:
        total, ready = halve(total, bit, ready)
        bit *= 2
    mixed, input_grad = ready
    weight_grad = total[0] / jnp.sqrt(F32(rows * nseq * ndp))
    return mixed[None], input_grad[None], weight_grad


def solution(mesh):
    placed = (
        P("dp", "seq", None),
        P("dp", None),
        P("dp", None),
        P("seq", None, None),
        P("seq", None, None),
        P("dp", "seq", None),
    )
    return jax.shard_map(
        on_device,
        mesh=mesh,
        in_specs=placed,
        out_specs=(P("dp", "seq", None), P("dp", "seq", None), P(("seq", "dp"), None)),
        check_vma=False,
    )
```
